512 devices in a mesh: replica: 16 (over y, z_lo), fsdp: 32 (over x, z_hi, core).
Axes of the slice: x: 4, y: 4, z: 16 (z_hi: 4, z_lo: 4; z = z_hi * 4 + z_lo), core: 2. Of those that a mesh axis runs over, the one named last changes fastest.
Arguments:
- previous_global_weights: float32 [4194304], P('fsdp')
- replica_local_weights: float32 [16, 4194304], P('replica', 'fsdp')
- momentum: float32 [64, 4194304], P(None, ('fsdp', 'replica')), may hold values from -4 to 4
- reporting_replica_tokens: int32 [16], replicated, may hold values from 0 to 4096, as said below
- target_fragment_index: int32 [1], replicated, may hold values from 0 to 63
Outputs:
- new_weights: float32 [4194304], P('fsdp')
- new_momentum: float32 [4194304], P(('fsdp', 'replica'))
The draws below stay inside these ranges and needn't reach their ends.
Inputs may be any that keep to these rules, and one draw needn't show every extreme that they name: `reporting_replica_tokens`: exactly one replica is lost and has 0 tokens; every other replica has 1024 or more.
All inputs are finite; a program needn't handle non-finite values.
Results may differ from the reference program's by a relative error of at most 0.000048.
Values sent between devices are 32-bit elements; how exact they have to be, the bound alone decides.
No kernel may reach another device: no remote copies, remote signals or barrier semaphores. Data moves between devices by JAX's collectives and lax.ppermute only.
A program may use at most 64 MiB of HBM per device.

```python
import math
import jax
import jax.numpy as jnp
from jax import lax

NFRAG = 64
FRAG = 4194304
N_REPLICA = 16


def scale_profile():
    position = jnp.arange(FRAG, dtype=jnp.float32) / FRAG
    return jnp.exp(position * math.log(10.0))


def draw_previous_global_weights(key, part):
    key = jax.random.fold_in(key, 11)
    values = jax.random.normal(key, (FRAG,), jnp.float32)
    return scale_profile() * values


def draw_replica_local_weights(key, part):
    key = jax.random.fold_in(key, 23)
    values = jax.random.normal(key, (N_REPLICA, FRAG), jnp.float32)
    return scale_profile()[None, :] * values


def draw_reporting_replica_tokens(key, part):
    key = jax.random.fold_in(key, 37)
    lost_key, count_key = jax.random.split(key)
    lost = jax.random.randint(lost_key, (), 0, N_REPLICA)
    counts = jax.random.randint(count_key, (N_REPLICA,), 1024, 4096)
    places = jnp.arange(N_REPLICA, dtype=jnp.int32)
    counts = jnp.where(places == (lost + 1) % N_REPLICA, 4096, counts)
    counts = jnp.where(places == lost, 0, counts)
    return counts.astype(jnp.int32)


def level_of(own_key, extent, cuts, least, largest):
    def one(dim, blocks):
        heights = jax.random.uniform(jax.random.fold_in(jax.random.fold_in(own_key, 6), dim), (blocks,), jnp.float32, least / len(cuts), largest / len(cuts))
        return jnp.repeat(jnp.exp(heights), extent[dim] // blocks).reshape((-1,) + (1,) * (len(extent) - dim - 1))

    factor_of = one(*cuts[0])
    for cut in cuts[1:]:
        factor_of = factor_of * one(*cut)
    return factor_of


def gaussian(stream_key, extent, width, reach, cuts=(), kind=jnp.bfloat16):
    drawn = width * jax.random.normal(stream_key, extent, jnp.float32)
    if cuts:
        drawn = drawn * level_of(stream_key, extent, cuts, -0.22, 0.18)
    return jnp.clip(drawn, -reach, reach).astype(kind)


def setup_inputs(seed: int = 0) -> dict:
    splits = jax.random.split(jax.random.key(seed), 6)
    previous_global_weights = draw_previous_global_weights(jax.random.fold_in(splits[5], 71), 0)
    replica_local_weights = draw_replica_local_weights(jax.random.fold_in(splits[5], 71), 0)
    momentum = gaussian(splits[2], (NFRAG, FRAG), 0.5, 4.0, ((1, 512),), jnp.float32)
    reporting_replica_tokens = draw_reporting_replica_tokens(jax.random.fold_in(splits[5], 71), 0)
    target_fragment_index = jax.random.randint(splits[4], (1,), 0, NFRAG).astype(jnp.int32)
    return {"previous_global_weights": previous_global_weights, "replica_local_weights": replica_local_weights, "momentum": momentum, "reporting_replica_tokens": reporting_replica_tokens, "target_fragment_index": target_fragment_index}


beta_outer = 0.9
rate_outer = 0.7
clip_scale = 2.0
epsilon = 1e-06

def reference(previous_global_weights, replica_local_weights, momentum, reporting_replica_tokens, target_fragment_index):
    replica_token_weights = reporting_replica_tokens.astype(jnp.float32)

    def accumulate(index, masked_weight_total):
        return masked_weight_total + replica_token_weights[index] * (previous_global_weights - replica_local_weights[index])
    masked_weight_total = lax.fori_loop(0, N_REPLICA, accumulate, jnp.zeros((FRAG,), jnp.float32))
    mean_replica_weights = masked_weight_total / jnp.sum(replica_token_weights)
    grad_norm = jnp.sqrt(jnp.sum(mean_replica_weights * mean_replica_weights) + epsilon)
    clipped = mean_replica_weights * jnp.minimum(1.0, clip_scale * math.sqrt(FRAG) / grad_norm)
    state_row = lax.dynamic_index_in_dim(momentum, target_fragment_index[0], 0, keepdims=False)
    new_momentum = beta_outer * state_row + clipped
    new_weights = previous_global_weights - rate_outer * (beta_outer * new_momentum + clipped)
    return (new_weights, new_momentum)
```

```python
import math

import jax
import jax.numpy as jnp
from jax import lax
from jax.sharding import PartitionSpec as P

beta_outer = 0.9
rate_outer = 0.7
clip_scale = 2.0
epsilon = 1e-06
lanes = 128


def cross_groups(replicas, shards):
    def at(x, y, z, core):
        return (y * 4 + z % 4) * shards + x * 8 + (z // 4) * 2 + core

    planes = [
        [at(x, y, z, core) for x in range(4) for y in range(4)]
        for z in range(16)
        for core in range(2)
    ]
    columns = [
        [at(x, y, z, core) for z in range(16) for core in range(2)]
        for x in range(4)
        for y in range(4)
    ]
    return planes, columns


def group_sum(value, groups):
    spread = jnp.broadcast_to(value, (len(groups[0]), 1, lanes))
    parts = lax.all_to_all(
        spread, ("replica", "fsdp"), 0, 0, axis_index_groups=groups, tiled=True
    )
    return jnp.sum(parts[:, 0, 0])


def share(piece, count):
    spread = jnp.broadcast_to(piece[None], (count,) + piece.shape)
    return lax.all_to_all(spread, "replica", 0, 0, tiled=True)


def local(
    previous_global_weights,
    replica_local_weights,
    momentum,
    reporting_replica_tokens,
    target_fragment_index,
):
    replicas = lax.axis_size("replica")
    shards = lax.axis_size("fsdp")
    replica_pos = lax.axis_index("replica")
    frag_total = previous_global_weights.shape[0] * shards
    limit = clip_scale * math.sqrt(frag_total)
    token_weights = reporting_replica_tokens.astype(jnp.float32)
    reporting_count = jnp.sum(token_weights)
    blocks = previous_global_weights.reshape(replicas, -1, lanes)
    pieces = lax.all_to_all(
        replica_local_weights[0].reshape(blocks.shape), "replica", 0, 0, tiled=True
    )
    old_piece = lax.dynamic_index_in_dim(blocks, replica_pos, 0, keepdims=False)
    state = lax.dynamic_index_in_dim(momentum, target_fragment_index[0], 0, keepdims=False)
    state_piece = state.reshape(old_piece.shape)
    total = jnp.sum(token_weights[:, None, None] * (old_piece[None] - pieces), 0)
    average = total / reporting_count
    planes, columns = cross_groups(replicas, shards)
    squares = jnp.sum(average * average)
    squares = group_sum(squares, planes)
    squares = group_sum(squares, columns)
    all_state = share(state_piece, replicas)
    all_average = share(average, replicas)
    scale = jnp.minimum(1.0, limit / jnp.sqrt(squares + epsilon))
    new_momentum = beta_outer * state_piece + average * scale
    clipped = all_average * scale
    step = beta_outer * (beta_outer * all_state + clipped) + clipped
    new_weights = blocks - rate_outer * step
    return (new_weights.reshape(-1), new_momentum.reshape(-1))


def solution(mesh):
    placed = (P("fsdp"), P("replica", "fsdp"), P(None, ("fsdp", "replica")), P(), P())
    return jax.shard_map(
        local,
        mesh=mesh,
        in_specs=placed,
        out_specs=(P("fsdp"), P(("fsdp", "replica"))),
        check_vma=False,
    )
```

```python
import math

import jax
import jax.numpy as jnp
from jax import lax
from jax.sharding import PartitionSpec as P

beta_outer = 0.9
rate_outer = 0.7
clip_scale = 2.0
epsilon = 1e-06
lanes = 128


def line_groups(replicas):
    along_y = [[y * 4 + z for y in range(4)] for z in range(4)]
    along_z = [[y * 4 + z for z in range(4)] for y in range(4)]
    return along_y, along_z


def local(
    previous_global_weights,
    replica_local_weights,
    momentum,
    reporting_replica_tokens,
    target_fragment_index,
):
    replicas = lax.axis_size("replica")
    shards = lax.axis_size("fsdp")
    replica_pos = lax.axis_index("replica")
    row, column = replica_pos // 4, replica_pos % 4
    frag_total = previous_global_weights.shape[0] * shards
    limit = clip_scale * math.sqrt(frag_total)
    along_y, along_z = line_groups(replicas)
    token_weights = reporting_replica_tokens.astype(jnp.float32)
    reporting_count = jnp.sum(token_weights)
    blocks = previous_global_weights.reshape(4, -1, lanes)
    depth = blocks.shape[1]
    old_block = lax.dynamic_index_in_dim(blocks, row, 0, keepdims=False)
    state = lax.dynamic_index_in_dim(momentum, target_fragment_index[0], 0, keepdims=False)
    state_piece = state.reshape(-1, lanes)
    column_weights = lax.dynamic_index_in_dim(token_weights.reshape(4, 4), column, 1, keepdims=False)
    received = lax.all_to_all(
        replica_local_weights[0].reshape(blocks.shape), "replica", 0, 0, axis_index_groups=along_y, tiled=True
    )
    partial = jnp.sum(column_weights[:, None, None] * (old_block[None] - received), 0)

    sent = jnp.concatenate([partial, state_piece], 0)
    parts = lax.all_gather(sent, "replica", axis=0, axis_index_groups=along_z)
    average = jnp.sum(parts[:, :depth], 0) / reporting_count
    state_block = parts[:, depth:].reshape(depth, lanes)
    squares = jnp.broadcast_to(jnp.sum(average * average), (8, lanes))
    sent = jnp.concatenate([average, state_block, squares], 0)
    sent = jnp.broadcast_to(sent[None], (4,) + sent.shape)
    parts = lax.all_to_all(sent, "replica", 0, 0, axis_index_groups=along_y, tiled=True)
    squares = jnp.sum(parts[:, 2 * depth, 0])
    parts_f = lax.all_to_all(jnp.broadcast_to(squares, (shards, 1, lanes)), "fsdp", 0, 0, tiled=True)
    squares = jnp.sum(parts_f[:, 0, 0])
    scale = jnp.minimum(1.0, limit / jnp.sqrt(squares + epsilon))
    own = lax.dynamic_slice_in_dim(average, column * (depth // 4), depth // 4, 0)
    new_momentum = beta_outer * state_piece + own * scale
    clipped = parts[:, :depth] * scale
    step = beta_outer * (beta_outer * parts[:, depth : 2 * depth] + clipped) + clipped
    new_weights = blocks - rate_outer * step
    return (new_weights.reshape(-1), new_momentum.reshape(-1))


def solution(mesh):
    placed = (P("fsdp"), P("replica", "fsdp"), P(None, ("fsdp", "replica")), P(), P())
    return jax.shard_map(
        local,
        mesh=mesh,
        in_specs=placed,
        out_specs=(P("fsdp"), P(("fsdp", "replica"))),
        check_vma=False,
    )
```

```python
import math

import jax
import jax.numpy as jnp
from jax import lax
from jax.sharding import PartitionSpec as P

beta_outer = 0.9
rate_outer = 0.7
clip_scale = 2.0
epsilon = 1e-06
lanes = 128


def scalar_groups(shards):
    near = [
        [(y * 4 + z) * shards + x * 8 + far * 2 + core for y in range(4) for x in range(4) for core in range(2)]
        for z in range(4)
        for far in range(4)
    ]
    far = [[x * 8 + z * 2 + core for z in range(4)] for x in range(4) for core in range(2)]
    return near, far


def line_groups(replicas):
    along_y = [[y * 4 + z for y in range(4)] for z in range(4)]
    along_z = [[y * 4 + z for z in range(4)] for y in range(4)]
    return along_y, along_z


def local(
    previous_global_weights,
    replica_local_weights,
    momentum,
    reporting_replica_tokens,
    target_fragment_index,
):
    replicas = lax.axis_size("replica")
    shards = lax.axis_size("fsdp")
    replica_pos = lax.axis_index("replica")
    row, column = replica_pos // 4, replica_pos % 4
    frag_total = previous_global_weights.shape[0] * shards
    limit = clip_scale * math.sqrt(frag_total)
    along_y, along_z = line_groups(replicas)
    token_weights = reporting_replica_tokens.astype(jnp.float32)
    reporting_count = jnp.sum(token_weights)
    blocks = previous_global_weights.reshape(4, -1, lanes)
    depth = blocks.shape[1]
    old_block = lax.dynamic_index_in_dim(blocks, row, 0, keepdims=False)
    state = lax.dynamic_index_in_dim(momentum, target_fragment_index[0], 0, keepdims=False)
    state_piece = state.reshape(-1, lanes)
    column_weights = lax.dynamic_index_in_dim(token_weights.reshape(4, 4), column, 1, keepdims=False)
    received = lax.all_to_all(
        replica_local_weights[0].reshape(blocks.shape), "replica", 0, 0, axis_index_groups=along_y, tiled=True
    )
    partial = jnp.sum(column_weights[:, None, None] * (old_block[None] - received), 0)

    sent = jnp.concatenate([partial, state_piece], 0)
    parts = lax.all_gather(sent, "replica", axis=0, axis_index_groups=along_z)
    average = jnp.sum(parts[:, :depth], 0) / reporting_count
    state_block = parts[:, depth:].reshape(depth, lanes)
    near, far = scalar_groups(shards)
    squares = jnp.broadcast_to(jnp.sum(average * average), (len(near[0]), 1, lanes))
    squares = lax.all_to_all(squares, ("replica", "fsdp"), 0, 0, axis_index_groups=near, tiled=True)
    squares = jnp.sum(squares[:, 0, 0])
    sent = jnp.concatenate([average, state_block], 0)
    sent, squares = lax.optimization_barrier((sent, squares))
    sent = jnp.broadcast_to(sent[None], (4,) + sent.shape)
    parts = lax.all_to_all(sent, "replica", 0, 0, axis_index_groups=along_y, tiled=True)
    squares = lax.psum(squares, "fsdp", axis_index_groups=far)
    scale = jnp.minimum(1.0, limit / jnp.sqrt(squares + epsilon))
    own = lax.dynamic_slice_in_dim(average, column * (depth // 4), depth // 4, 0)
    new_momentum = beta_outer * state_piece + own * scale
    clipped = parts[:, :depth] * scale
    step = beta_outer * (beta_outer * parts[:, depth : 2 * depth] + clipped) + clipped
    new_weights = blocks - rate_outer * step
    return (new_weights.reshape(-1), new_momentum.reshape(-1))


def solution(mesh):
    placed = (P("fsdp"), P("replica", "fsdp"), P(None, ("fsdp", "replica")), P(), P())
    return jax.shard_map(
        local,
        mesh=mesh,
        in_specs=placed,
        out_specs=(P("fsdp"), P(("fsdp", "replica"))),
        check_vma=False,
    )
```

```python
import math

import jax
import jax.numpy as jnp
from jax import lax
from jax.sharding import PartitionSpec as P

beta_outer = 0.9
rate_outer = 0.7
clip_scale = 2.0
epsilon = 1e-06
lanes = 128


def block_groups():
    return [[y * 4 + half * 2 + side for y in range(4) for side in range(2)] for half in range(2)]


def line_groups():
    return [[y * 4 + z for y in range(4)] for z in range(4)]


def near_groups(shards):
    return [
        [
            (y * 4 + half * 2 + side) * shards + x * 8 + far * 2 + core
            for y in range(4)
            for side in range(2)
            for x in range(4)
            for core in range(2)
        ]
        for half in range(2)
        for far in range(4)
    ]


def far_groups():
    return [[x * 8 + far * 2 + core for far in range(4)] for x in range(4) for core in range(2)]


def local(
    previous_global_weights,
    replica_local_weights,
    momentum,
    reporting_replica_tokens,
    target_fragment_index,
):
    replicas = lax.axis_size("replica")
    shards = lax.axis_size("fsdp")
    replica_pos = lax.axis_index("replica")
    row, half, side = replica_pos >> 2, (replica_pos >> 1) & 1, replica_pos & 1
    frag_total = previous_global_weights.shape[0] * shards
    limit = clip_scale * math.sqrt(frag_total)
    token_weights = reporting_replica_tokens.astype(jnp.float32)
    reporting_count = jnp.sum(token_weights)
    blocks = previous_global_weights.reshape(8, -1, lanes)
    depth = blocks.shape[1]
    old_block = lax.dynamic_index_in_dim(blocks, row * 2 + side, 0, keepdims=False)
    state = lax.dynamic_index_in_dim(momentum, target_fragment_index[0], 0, keepdims=False)
    state_piece = state.reshape(-1, lanes)
    group_weights = lax.dynamic_index_in_dim(
        token_weights.reshape(4, 2, 2), half, 1, keepdims=False
    ).reshape(8)
    received = lax.all_to_all(
        replica_local_weights[0].reshape(blocks.shape),
        "replica", 0, 0, axis_index_groups=block_groups(), tiled=True,
    )
    partial = jnp.sum(group_weights[:, None, None] * (old_block[None] - received), 0)
    sent = jnp.concatenate([partial, state_piece], 0)
    other = lax.ppermute(sent, "replica", [(i, i ^ 2) for i in range(replicas)])
    average = (partial + other[:depth]) / reporting_count
    pair = jnp.stack([state_piece, other[depth:]])
    pair = jnp.where(half == 0, pair, pair[::-1]).reshape(depth, lanes)
    near = near_groups(shards)
    squares = jnp.broadcast_to(jnp.sum(average * average), (len(near[0]), 1, lanes))
    mine = jnp.concatenate([average, pair], 0)
    beside = lax.ppermute(mine, "replica", [(i, i ^ 1) for i in range(replicas)])
    squares = lax.all_to_all(squares, ("replica", "fsdp"), 0, 0, axis_index_groups=near, tiled=True)
    squares = jnp.sum(squares[:, 0, 0])
    sent = jnp.where(side == 0, jnp.stack([mine, beside]), jnp.stack([beside, mine]))
    sent, squares = lax.optimization_barrier((sent, squares))
    sent = jnp.broadcast_to(sent[None], (4,) + sent.shape)
    parts = lax.all_to_all(sent, "replica", 0, 0, axis_index_groups=line_groups(), tiled=True)
    parts = parts.reshape(8, -1, lanes)
    squares = lax.psum(squares, "fsdp", axis_index_groups=far_groups())
    scale = jnp.minimum(1.0, limit / jnp.sqrt(squares + epsilon))
    pieces = parts[:, :depth].reshape(replicas, -1, lanes)
    own = lax.dynamic_index_in_dim(pieces, replica_pos, 0, keepdims=False)
    new_momentum = beta_outer * state_piece + own * scale
    clipped = pieces * scale
    all_state = parts[:, depth:].reshape(4, 2, 2, -1, lanes).swapaxes(1, 2).reshape(pieces.shape)
    step = beta_outer * (beta_outer * all_state + clipped) + clipped
    new_weights = blocks.reshape(pieces.shape) - rate_outer * step
    return (new_weights.reshape(-1), new_momentum.reshape(-1))


def solution(mesh):
    placed = (P("fsdp"), P("replica", "fsdp"), P(None, ("fsdp", "replica")), P(), P())
    return jax.shard_map(
        local,
        mesh=mesh,
        in_specs=placed,
        out_specs=(P("fsdp"), P(("fsdp", "replica"))),
        check_vma=False,
    )
```

```python
import math

import jax
import jax.numpy as jnp
from jax import lax
from jax.sharding import PartitionSpec as P

beta_outer = 0.9
rate_outer = 0.7
clip_scale = 2.0
epsilon = 1e-06
lanes = 128


def block_groups():
    return [[y * 4 + half * 2 + side for y in range(4) for side in range(2)] for half in range(2)]


def line_groups():
    return [[y * 4 + z for y in range(4)] for z in range(4)]


def near_groups(shards):
    return [
        [
            (y * 4 + half * 2 + side) * shards + x * 8 + far * 2 + core
            for y in range(4)
            for side in range(2)
            for x in range(4)
            for core in range(2)
        ]
        for half in range(2)
        for far in range(4)
    ]


def far_groups():
    return [[x * 8 + far * 2 + core for far in range(4)] for x in range(4) for core in range(2)]


def local(
    previous_global_weights,
    replica_local_weights,
    momentum,
    reporting_replica_tokens,
    target_fragment_index,
):
    replicas = lax.axis_size("replica")
    shards = lax.axis_size("fsdp")
    replica_pos = lax.axis_index("replica")
    row, half, side = replica_pos >> 2, (replica_pos >> 1) & 1, replica_pos & 1
    frag_total = previous_global_weights.shape[0] * shards
    limit = clip_scale * math.sqrt(frag_total)
    token_weights = reporting_replica_tokens.astype(jnp.float32)
    token_shares = token_weights / jnp.sum(token_weights)
    blocks = previous_global_weights.reshape(8, -1, lanes)
    depth = blocks.shape[1]
    old_block = lax.dynamic_index_in_dim(blocks, row * 2 + side, 0, keepdims=False)
    state = lax.dynamic_index_in_dim(momentum, target_fragment_index[0], 0, keepdims=False)
    state_piece = state.reshape(-1, lanes)
    group_shares = lax.dynamic_index_in_dim(
        token_shares.reshape(4, 2, 2), half, 1, keepdims=False
    ).reshape(8)
    received = lax.all_to_all(
        replica_local_weights[0].reshape(blocks.shape),
        "replica", 0, 0, axis_index_groups=block_groups(), tiled=True,
    )
    partial = jnp.sum(group_shares[:, None, None] * (old_block[None] - received), 0)
    sent = jnp.concatenate([partial, state_piece], 0)
    other = lax.ppermute(sent, "replica", [(i, i ^ 2) for i in range(replicas)])
    average = partial + other[:depth]
    pair = jnp.stack([state_piece, other[depth:]])
    pair = jnp.where(half == 0, pair, pair[::-1]).reshape(depth, lanes)
    near = near_groups(shards)
    rows = jnp.sum(average * average, 0, keepdims=True)
    rows = jnp.dot(rows, jnp.ones((lanes, lanes), jnp.float32), precision=lax.Precision.HIGHEST)
    squares = jnp.broadcast_to(rows[None], (len(near[0]), 1, lanes))
    mine = jnp.concatenate([average, pair], 0)
    beside = lax.ppermute(mine, "replica", [(i, i ^ 1) for i in range(replicas)])
    squares = lax.all_to_all(squares, ("replica", "fsdp"), 0, 0, axis_index_groups=near, tiled=True)
    squares = jnp.sum(squares[:, 0, 0])
    sent = jnp.where(side == 0, jnp.stack([mine, beside]), jnp.stack([beside, mine]))
    sent, squares = lax.optimization_barrier((sent, squares))
    sent = jnp.broadcast_to(sent[None], (4,) + sent.shape)
    parts = lax.all_to_all(sent, "replica", 0, 0, axis_index_groups=line_groups(), tiled=True)
    parts = parts.reshape(8, -1, lanes)
    squares = lax.psum(squares, "fsdp", axis_index_groups=far_groups())
    scale = jnp.minimum(1.0, limit / jnp.sqrt(squares + epsilon))
    pieces = parts[:, :depth].reshape(replicas, -1, lanes)
    own = lax.dynamic_index_in_dim(pieces, replica_pos, 0, keepdims=False)
    new_momentum = beta_outer * state_piece + own * scale
    clipped = pieces * scale
    all_state = parts[:, depth:].reshape(4, 2, 2, -1, lanes).swapaxes(1, 2).reshape(pieces.shape)
    step = beta_outer * (beta_outer * all_state + clipped) + clipped
    new_weights = blocks.reshape(pieces.shape) - rate_outer * step
    return (new_weights.reshape(-1), new_momentum.reshape(-1))


def solution(mesh):
    placed = (P("fsdp"), P("replica", "fsdp"), P(None, ("fsdp", "replica")), P(), P())
    return jax.shard_map(
        local,
        mesh=mesh,
        in_specs=placed,
        out_specs=(P("fsdp"), P(("fsdp", "replica"))),
        check_vma=False,
    )
```

```python
import math

import jax
import jax.numpy as jnp
from jax import lax
from jax.sharding import PartitionSpec as P

beta_outer = 0.9
rate_outer = 0.7
clip_scale = 2.0
epsilon = 1e-06
lanes = 128


def block_groups():
    return [[y * 4 + half * 2 + side for y in range(4) for side in range(2)] for half in range(2)]


def line_groups():
    return [[y * 4 + z for y in range(4)] for z in range(4)]


def near_groups(shards):
    return [
        [
            (y * 4 + half * 2 + side) * shards + x * 8 + far * 2 + core
            for y in range(4)
            for side in range(2)
            for x in range(4)
            for core in range(2)
        ]
        for half in range(2)
        for far in range(4)
    ]


def far_groups():
    return [[x * 8 + far * 2 + core for far in range(4)] for x in range(4) for core in range(2)]


def lane_total(row):
    ones = jnp.ones((lanes, lanes), jnp.float32)
    total = jnp.dot(row * 2.0**-40, ones, precision=lax.Precision.HIGHEST) * 2.0**40
    return jnp.where(jnp.isnan(total), jnp.inf, total)


def local(
    previous_global_weights,
    replica_local_weights,
    momentum,
    reporting_replica_tokens,
    target_fragment_index,
):
    replicas = lax.axis_size("replica")
    shards = lax.axis_size("fsdp")
    replica_pos = lax.axis_index("replica")
    row, half, side = replica_pos >> 2, (replica_pos >> 1) & 1, replica_pos & 1
    frag_total = previous_global_weights.shape[0] * shards
    limit = clip_scale * math.sqrt(frag_total)
    token_weights = reporting_replica_tokens.astype(jnp.float32)
    ones = jnp.ones((replicas, replicas), jnp.float32)
    counts = jnp.dot(token_weights[None], ones, precision=lax.Precision.HIGHEST)
    token_shares = token_weights / counts[0]
    blocks = previous_global_weights.reshape(8, -1, lanes)
    depth = blocks.shape[1]
    old_block = lax.dynamic_index_in_dim(blocks, row * 2 + side, 0, keepdims=False)
    state = lax.dynamic_index_in_dim(momentum, target_fragment_index[0], 0, keepdims=False)
    state_piece = state.reshape(-1, lanes)
    group_shares = lax.dynamic_index_in_dim(
        token_shares.reshape(4, 2, 2), half, 1, keepdims=False
    ).reshape(8)
    other_state = lax.ppermute(state_piece, "replica", [(i, i ^ 2) for i in range(replicas)])
    received = lax.all_to_all(
        replica_local_weights[0].reshape(blocks.shape),
        "replica", 0, 0, axis_index_groups=block_groups(), tiled=True,
    )
    partial = jnp.sum(group_shares[:, None, None] * (old_block[None] - received), 0)
    average = partial + lax.ppermute(partial, "replica", [(i, i ^ 2) for i in range(replicas)])
    pair = jnp.stack([state_piece, other_state])
    pair = jnp.where(half == 0, pair, pair[::-1]).reshape(depth, lanes)
    near = near_groups(shards)
    squares = lane_total(jnp.sum(average * average, 0, keepdims=True))
    squares = jnp.broadcast_to(squares[None], (len(near[0]), 1, lanes))
    mine = jnp.concatenate([average, pair], 0)
    beside = lax.ppermute(mine, "replica", [(i, i ^ 1) for i in range(replicas)])
    squares = lax.all_to_all(squares, ("replica", "fsdp"), 0, 0, axis_index_groups=near, tiled=True)
    squares = jnp.sum(squares[:32, 0] + squares[32:, 0], 0, keepdims=True)
    sent = jnp.where(side == 0, jnp.stack([mine, beside]), jnp.stack([beside, mine]))
    sent, squares = lax.optimization_barrier((sent, squares))
    sent = jnp.broadcast_to(sent[None], (4,) + sent.shape)
    parts = lax.all_to_all(sent, "replica", 0, 0, axis_index_groups=line_groups(), tiled=True)
    parts = parts.reshape(8, -1, lanes)
    squares = lax.psum(squares, "fsdp", axis_index_groups=far_groups())
    scale = jnp.minimum(1.0, limit / jnp.sqrt(squares + epsilon))
    pieces = parts[:, :depth].reshape(replicas, -1, lanes)
    own = lax.dynamic_index_in_dim(pieces, replica_pos, 0, keepdims=False)
    new_momentum = beta_outer * state_piece + own * scale
    clipped = pieces * scale
    all_state = parts[:, depth:].reshape(4, 2, 2, -1, lanes).swapaxes(1, 2).reshape(pieces.shape)
    step = beta_outer * (beta_outer * all_state + clipped) + clipped
    new_weights = blocks.reshape(pieces.shape) - rate_outer * step
    return (new_weights.reshape(-1), new_momentum.reshape(-1))


def solution(mesh):
    placed = (P("fsdp"), P("replica", "fsdp"), P(None, ("fsdp", "replica")), P(), P())
    return jax.shard_map(
        local,
        mesh=mesh,
        in_specs=placed,
        out_specs=(P("fsdp"), P(("fsdp", "replica"))),
        check_vma=False,
    )
```

```python
import math

import jax
import jax.numpy as jnp
from jax import lax
from jax.sharding import PartitionSpec as P

beta_outer = 0.9
rate_outer = 0.7
clip_scale = 2.0
epsilon = 1e-06
lanes = 128


def block_groups():
    return [[y * 4 + half * 2 + side for y in range(4) for side in range(2)] for half in range(2)]


def line_groups():
    return [[y * 4 + z for y in range(4)] for z in range(4)]


def near_groups(shards):
    return [
        [
            (y * 4 + half * 2 + side) * shards + x * 8 + far * 2 + core
            for y in range(4)
            for side in range(2)
            for x in range(4)
            for core in range(2)
        ]
        for half in range(2)
        for far in range(4)
    ]


def far_groups():
    return [[x * 8 + far * 2 + core for far in range(4)] for x in range(4) for core in range(2)]


def lane_total(row):
    ones = jnp.ones((lanes, lanes), jnp.float32)
    total = jnp.dot(row * 2.0**-40, ones, precision=lax.Precision.HIGHEST) * 2.0**40
    return jnp.where(jnp.isnan(total), jnp.inf, total)


def local(
    previous_global_weights,
    replica_local_weights,
    momentum,
    reporting_replica_tokens,
    target_fragment_index,
):
    replicas = lax.axis_size("replica")
    shards = lax.axis_size("fsdp")
    replica_pos = lax.axis_index("replica")
    row, half, side = replica_pos >> 2, (replica_pos >> 1) & 1, replica_pos & 1
    frag_total = previous_global_weights.shape[0] * shards
    limit = clip_scale * math.sqrt(frag_total)
    token_weights = reporting_replica_tokens.astype(jnp.float32)
    ones = jnp.ones((replicas, replicas), jnp.float32)
    counts = jnp.dot(token_weights[None], ones, precision=lax.Precision.HIGHEST)
    token_shares = token_weights / counts[0]
    blocks = previous_global_weights.reshape(8, -1, lanes)
    depth = blocks.shape[1]
    old_block = lax.dynamic_index_in_dim(blocks, row * 2 + side, 0, keepdims=False)
    state = lax.dynamic_index_in_dim(momentum, target_fragment_index[0], 0, keepdims=False)
    state_piece = state.reshape(-1, lanes)
    group_shares = lax.dynamic_index_in_dim(
        token_shares.reshape(4, 2, 2), half, 1, keepdims=False
    ).reshape(8)
    other_state = lax.ppermute(state_piece, "replica", [(i, i ^ 2) for i in range(replicas)])
    received = lax.all_to_all(
        replica_local_weights[0].reshape(blocks.shape),
        "replica", 0, 0, axis_index_groups=block_groups(), tiled=True,
    )
    partial = jnp.sum(group_shares[:, None, None] * (old_block[None] - received), 0)
    average = partial + lax.ppermute(partial, "replica", [(i, i ^ 2) for i in range(replicas)])
    other_state, _ = lax.optimization_barrier((other_state, partial))
    pair = jnp.stack([state_piece, other_state])
    pair = jnp.where(half == 0, pair, pair[::-1]).reshape(depth, lanes)
    beside_pair = lax.ppermute(pair, "replica", [(i, i ^ 1) for i in range(replicas)])
    near = near_groups(shards)
    squares = lane_total(jnp.sum(average * average, 0, keepdims=True))
    squares = jnp.broadcast_to(squares[None], (len(near[0]), 1, lanes))
    beside = lax.ppermute(average, "replica", [(i, i ^ 1) for i in range(replicas)])
    squares = lax.all_to_all(squares, ("replica", "fsdp"), 0, 0, axis_index_groups=near, tiled=True)
    squares = jnp.sum(squares[:32, 0] + squares[32:, 0], 0, keepdims=True)
    beside, squares = lax.optimization_barrier((beside, squares))
    first = side == 0
    averages = jnp.where(first, jnp.stack([average, beside]), jnp.stack([beside, average]))
    pairs = jnp.where(first, jnp.stack([pair, beside_pair]), jnp.stack([beside_pair, pair]))
    sent = jnp.concatenate([averages, pairs], 1)
    sent, squares = lax.optimization_barrier((sent, squares))
    sent = jnp.broadcast_to(sent[None], (4,) + sent.shape)
    parts = lax.all_to_all(sent, "replica", 0, 0, axis_index_groups=line_groups(), tiled=True)
    parts = parts.reshape(8, -1, lanes)
    squares = lax.psum(squares, "fsdp", axis_index_groups=far_groups())
    scale = jnp.minimum(1.0, limit / jnp.sqrt(squares + epsilon))
    pieces = parts[:, :depth].reshape(replicas, -1, lanes)
    own = lax.dynamic_index_in_dim(pieces, replica_pos, 0, keepdims=False)
    new_momentum = beta_outer * state_piece + own * scale
    clipped = pieces * scale
    all_state = parts[:, depth:].reshape(4, 2, 2, -1, lanes).swapaxes(1, 2).reshape(pieces.shape)
    step = beta_outer * (beta_outer * all_state + clipped) + clipped
    new_weights = blocks.reshape(pieces.shape) - rate_outer * step
    return (new_weights.reshape(-1), new_momentum.reshape(-1))


def solution(mesh):
    placed = (P("fsdp"), P("replica", "fsdp"), P(None, ("fsdp", "replica")), P(), P())
    return jax.shard_map(
        local,
        mesh=mesh,
        in_specs=placed,
        out_specs=(P("fsdp"), P(("fsdp", "replica"))),
        check_vma=False,
    )
```

```python
import functools
import math

import jax
import jax.numpy as jnp
from jax import lax
from jax.experimental import pallas as pl
from jax.experimental.pallas import tpu as pltpu
from jax.sharding import PartitionSpec as P

beta_outer = 0.9
rate_outer = 0.7
clip_scale = 2.0
epsilon = 1e-06
lanes = 128


def block_groups():
    return [[y * 4 + half * 2 + side for y in range(4) for side in range(2)] for half in range(2)]


def line_groups():
    return [[y * 4 + z for y in range(4)] for z in range(4)]


def near_groups(shards):
    return [
        [
            (y * 4 + half * 2 + side) * shards + x * 8 + far * 2 + core
            for y in range(4)
            for side in range(2)
            for x in range(4)
            for core in range(2)
        ]
        for half in range(2)
        for far in range(4)
    ]


def far_groups():
    return [[x * 8 + far * 2 + core for far in range(4)] for x in range(4) for core in range(2)]


def lane_total(row):
    ones = jnp.ones((lanes, lanes), jnp.float32)
    total = jnp.dot(row * 2.0**-40, ones, precision=lax.Precision.HIGHEST) * 2.0**40
    return jnp.where(jnp.isnan(total), jnp.inf, total)


def finish_kernel(
    limit, squares_ref, old_ref, parts_ref, own_ref, state_ref,
    new_ref, momentum_ref, new_buffer, momentum_buffer, new_sems, momentum_sem,
):
    depth = parts_ref.shape[1] // 2
    piece = depth // 2
    scale = jnp.minimum(1.0, limit / jnp.sqrt(squares_ref[...] + epsilon))
    momentum_buffer[...] = beta_outer * state_ref[...] + own_ref[...] * scale
    copies = [pltpu.make_async_copy(momentum_buffer, momentum_ref, momentum_sem)]
    copies[0].start()
    for y in range(4):
        for half in range(2):
            for side in range(2):
                clipped = parts_ref[y * 2 + half, side * piece : (side + 1) * piece] * scale
                state = parts_ref[y * 2 + side, depth + half * piece : depth + (half + 1) * piece]
                start = (y * 4 + half * 2 + side) * piece
                step = beta_outer * (beta_outer * state + clipped) + clipped
                new_buffer[start : start + piece] = old_ref[start : start + piece] - rate_outer * step
        chunk = pl.ds(y * 4 * piece, 4 * piece)
        copies.append(pltpu.make_async_copy(new_buffer.at[chunk], new_ref.at[chunk], new_sems.at[y]))
        copies[-1].start()
    for copy in copies:
        copy.wait()


def local(
    previous_global_weights,
    replica_local_weights,
    momentum,
    reporting_replica_tokens,
    target_fragment_index,
):
    replicas = lax.axis_size("replica")
    shards = lax.axis_size("fsdp")
    replica_pos = lax.axis_index("replica")
    row, half, side = replica_pos >> 2, (replica_pos >> 1) & 1, replica_pos & 1
    frag_total = previous_global_weights.shape[0] * shards
    limit = clip_scale * math.sqrt(frag_total)
    token_weights = reporting_replica_tokens.astype(jnp.float32)
    ones = jnp.ones((replicas, replicas), jnp.float32)
    counts = jnp.dot(token_weights[None], ones, precision=lax.Precision.HIGHEST)
    token_shares = token_weights / counts[0]
    blocks = previous_global_weights.reshape(8, -1, lanes)
    depth = blocks.shape[1]
    old_block = lax.dynamic_index_in_dim(blocks, row * 2 + side, 0, keepdims=False)
    state = lax.dynamic_index_in_dim(momentum, target_fragment_index[0], 0, keepdims=False)
    state_piece = state.reshape(-1, lanes)
    group_shares = lax.dynamic_index_in_dim(
        token_shares.reshape(4, 2, 2), half, 1, keepdims=False
    ).reshape(8)
    other_state = lax.ppermute(state_piece, "replica", [(i, i ^ 2) for i in range(replicas)])
    received = lax.all_to_all(
        replica_local_weights[0].reshape(blocks.shape),
        "replica", 0, 0, axis_index_groups=block_groups(), tiled=True,
    )
    partial = jnp.sum(group_shares[:, None, None] * (old_block[None] - received), 0)
    average = partial + lax.ppermute(partial, "replica", [(i, i ^ 2) for i in range(replicas)])
    other_state, _ = lax.optimization_barrier((other_state, partial))
    pair = jnp.stack([state_piece, other_state])
    pair = jnp.where(half == 0, pair, pair[::-1]).reshape(depth, lanes)
    beside_pair = lax.ppermute(pair, "replica", [(i, i ^ 1) for i in range(replicas)])
    near = near_groups(shards)
    squares = lane_total(jnp.sum(average * average, 0, keepdims=True))
    squares = jnp.broadcast_to(squares[None], (len(near[0]), 1, lanes))
    beside = lax.ppermute(average, "replica", [(i, i ^ 1) for i in range(replicas)])
    squares = lax.all_to_all(squares, ("replica", "fsdp"), 0, 0, axis_index_groups=near, tiled=True)
    squares = jnp.sum(squares[:32, 0] + squares[32:, 0], 0, keepdims=True)
    beside, squares = lax.optimization_barrier((beside, squares))
    first = side == 0
    averages = jnp.where(first, jnp.stack([average, beside]), jnp.stack([beside, average]))
    pairs = jnp.where(first, jnp.stack([pair, beside_pair]), jnp.stack([beside_pair, pair]))
    sent = jnp.concatenate([averages, pairs], 1)
    sent, squares = lax.optimization_barrier((sent, squares))
    sent = jnp.broadcast_to(sent[None], (4,) + sent.shape)
    parts = lax.all_to_all(sent, "replica", 0, 0, axis_index_groups=line_groups(), tiled=True)
    parts = parts.reshape(8, -1, lanes)
    squares = lax.psum(squares, "fsdp", axis_index_groups=far_groups())
    own = lax.dynamic_slice_in_dim(averages.reshape(-1, lanes), (replica_pos & 3) * (depth // 2), depth // 2)
    near_by = functools.partial(pltpu.with_memory_space_constraint, memory_space=pltpu.VMEM)
    vmem = pl.BlockSpec(memory_space=pltpu.VMEM)
    new_weights, new_momentum = pl.pallas_call(
        functools.partial(finish_kernel, limit),
        out_shape=(
            jax.ShapeDtypeStruct((8 * depth, lanes), jnp.float32),
            jax.ShapeDtypeStruct(state_piece.shape, jnp.float32),
        ),
        in_specs=[vmem] * 5,
        out_specs=(pl.BlockSpec(memory_space=pl.ANY), pl.BlockSpec(memory_space=pl.ANY)),
        scratch_shapes=[
            pltpu.VMEM((8 * depth, lanes), jnp.float32),
            pltpu.VMEM(state_piece.shape, jnp.float32),
            pltpu.SemaphoreType.DMA((4,)),
            pltpu.SemaphoreType.DMA,
        ],
        name="finish",
    )(near_by(squares), near_by(blocks.reshape(-1, lanes)), near_by(parts), near_by(own), near_by(state_piece))
    return (new_weights.reshape(-1), new_momentum.reshape(-1))


def solution(mesh):
    placed = (P("fsdp"), P("replica", "fsdp"), P(None, ("fsdp", "replica")), P(), P())
    return jax.shard_map(
        local,
        mesh=mesh,
        in_specs=placed,
        out_specs=(P("fsdp"), P(("fsdp", "replica"))),
        check_vma=False,
    )
```

```python
import functools
import math

import jax
import jax.numpy as jnp
from jax import lax
from jax.experimental import pallas as pl
from jax.experimental.pallas import tpu as pltpu
from jax.sharding import PartitionSpec as P

beta_outer = 0.9
rate_outer = 0.7
clip_scale = 2.0
epsilon = 1e-06
lanes = 128


def block_groups():
    return [[y * 4 + half * 2 + side for y in range(4) for side in range(2)] for half in range(2)]


def line_groups():
    return [[y * 4 + z for y in range(4)] for z in range(4)]


def near_groups(shards):
    return [
        [
            (y * 4 + half * 2 + side) * shards + x * 8 + far * 2 + core
            for y in range(4)
            for side in range(2)
            for x in range(4)
            for core in range(2)
        ]
        for half in range(2)
        for far in range(4)
    ]


def far_groups():
    return [[x * 8 + far * 2 + core for far in range(4)] for x in range(4) for core in range(2)]


def finish_kernel(
    limit, squares_ref, old_ref, parts_ref, own_ref, state_ref,
    new_ref, momentum_ref, new_buffer, momentum_buffer, new_sems, momentum_sem,
):
    depth = parts_ref.shape[1] // 2
    piece = depth // 2
    scale = jnp.minimum(1.0, limit / jnp.sqrt(jnp.sum(squares_ref[...], keepdims=True) + epsilon))
    momentum_buffer[...] = beta_outer * state_ref[...] + own_ref[...] * scale
    copies = [pltpu.make_async_copy(momentum_buffer, momentum_ref, momentum_sem)]
    copies[0].start()
    for y in range(4):
        for half in range(2):
            for side in range(2):
                clipped = parts_ref[y * 2 + half, side * piece : (side + 1) * piece] * scale
                state = parts_ref[y * 2 + side, depth + half * piece : depth + (half + 1) * piece]
                start = (y * 4 + half * 2 + side) * piece
                step = beta_outer * (beta_outer * state + clipped) + clipped
                new_buffer[start : start + piece] = old_ref[start : start + piece] - rate_outer * step
        chunk = pl.ds(y * 4 * piece, 4 * piece)
        copies.append(pltpu.make_async_copy(new_buffer.at[chunk], new_ref.at[chunk], new_sems.at[y]))
        copies[-1].start()
    for copy in copies:
        copy.wait()


def local(
    previous_global_weights,
    replica_local_weights,
    momentum,
    reporting_replica_tokens,
    target_fragment_index,
):
    replicas = lax.axis_size("replica")
    shards = lax.axis_size("fsdp")
    replica_pos = lax.axis_index("replica")
    row, half, side = replica_pos >> 2, (replica_pos >> 1) & 1, replica_pos & 1
    frag_total = previous_global_weights.shape[0] * shards
    limit = clip_scale * math.sqrt(frag_total)
    token_weights = reporting_replica_tokens.astype(jnp.float32)
    ones = jnp.ones((replicas, replicas), jnp.float32)
    counts = jnp.dot(token_weights[None], ones, precision=lax.Precision.HIGHEST)
    token_shares = token_weights / counts[0]
    blocks = previous_global_weights.reshape(8, -1, lanes)
    depth = blocks.shape[1]
    old_block = lax.dynamic_index_in_dim(blocks, row * 2 + side, 0, keepdims=False)
    state = lax.dynamic_index_in_dim(momentum, target_fragment_index[0], 0, keepdims=False)
    state_piece = state.reshape(-1, lanes)
    group_shares = lax.dynamic_index_in_dim(
        token_shares.reshape(4, 2, 2), half, 1, keepdims=False
    ).reshape(8)
    other_state = lax.ppermute(state_piece, "replica", [(i, i ^ 2) for i in range(replicas)])
    received = lax.all_to_all(
        replica_local_weights[0].reshape(blocks.shape),
        "replica", 0, 0, axis_index_groups=block_groups(), tiled=True,
    )
    partial = jnp.sum(group_shares[:, None, None] * (old_block[None] - received), 0)
    average = partial + lax.ppermute(partial, "replica", [(i, i ^ 2) for i in range(replicas)])
    other_state, _ = lax.optimization_barrier((other_state, partial))
    pair = jnp.stack([state_piece, other_state])
    pair = jnp.where(half == 0, pair, pair[::-1]).reshape(depth, lanes)
    beside_pair = lax.ppermute(pair, "replica", [(i, i ^ 1) for i in range(replicas)])
    near = near_groups(shards)
    squares = jnp.sum(average * average, 0, keepdims=True)
    squares = jnp.broadcast_to(squares[None], (len(near[0]), 1, lanes))
    beside = lax.ppermute(average, "replica", [(i, i ^ 1) for i in range(replicas)])
    squares = lax.all_to_all(squares, ("replica", "fsdp"), 0, 0, axis_index_groups=near, tiled=True)
    squares = jnp.sum((squares[:32, 0] + squares[32:, 0]).reshape(4, 8, lanes), 0)
    beside, squares = lax.optimization_barrier((beside, squares))
    first = side == 0
    averages = jnp.where(first, jnp.stack([average, beside]), jnp.stack([beside, average]))
    pairs = jnp.where(first, jnp.stack([pair, beside_pair]), jnp.stack([beside_pair, pair]))
    sent = jnp.concatenate([averages, pairs], 1)
    sent, squares = lax.optimization_barrier((sent, squares))
    sent = jnp.broadcast_to(sent[None], (4,) + sent.shape)
    parts = lax.all_to_all(sent, "replica", 0, 0, axis_index_groups=line_groups(), tiled=True)
    parts = parts.reshape(8, -1, lanes)
    squares = lax.psum(squares, "fsdp", axis_index_groups=far_groups())
    own = lax.dynamic_slice_in_dim(averages.reshape(-1, lanes), (replica_pos & 3) * (depth // 2), depth // 2)
    near_by = functools.partial(pltpu.with_memory_space_constraint, memory_space=pltpu.VMEM)
    vmem = pl.BlockSpec(memory_space=pltpu.VMEM)
    new_weights, new_momentum = pl.pallas_call(
        functools.partial(finish_kernel, limit),
        out_shape=(
            jax.ShapeDtypeStruct((8 * depth, lanes), jnp.float32),
            jax.ShapeDtypeStruct(state_piece.shape, jnp.float32),
        ),
        in_specs=[vmem] * 5,
        out_specs=(pl.BlockSpec(memory_space=pl.ANY), pl.BlockSpec(memory_space=pl.ANY)),
        scratch_shapes=[
            pltpu.VMEM((8 * depth, lanes), jnp.float32),
            pltpu.VMEM(state_piece.shape, jnp.float32),
            pltpu.SemaphoreType.DMA((4,)),
            pltpu.SemaphoreType.DMA,
        ],
        name="finish",
    )(near_by(squares), near_by(blocks.reshape(-1, lanes)), near_by(parts), near_by(own), near_by(state_piece))
    return (new_weights.reshape(-1), new_momentum.reshape(-1))


def solution(mesh):
    placed = (P("fsdp"), P("replica", "fsdp"), P(None, ("fsdp", "replica")), P(), P())
    return jax.shard_map(
        local,
        mesh=mesh,
        in_specs=placed,
        out_specs=(P("fsdp"), P(("fsdp", "replica"))),
        check_vma=False,
    )
```

```python
import functools
import math

import jax
import jax.numpy as jnp
from jax import lax
from jax.experimental import pallas as pl
from jax.experimental.pallas import tpu as pltpu
from jax.sharding import PartitionSpec as P

beta_outer = 0.9
rate_outer = 0.7
clip_scale = 2.0
epsilon = 1e-06
lanes = 128


def block_groups():
    return [[y * 4 + half * 2 + side for y in range(4) for side in range(2)] for half in range(2)]


def line_groups():
    return [[y * 4 + z for y in range(4)] for z in range(4)]


def near_groups(shards):
    return [
        [
            (y * 4 + half * 2 + side) * shards + x * 8 + far * 2 + core
            for y in range(4)
            for side in range(2)
            for x in range(4)
            for core in range(2)
        ]
        for half in range(2)
        for far in range(4)
    ]


def far_groups():
    return [[x * 8 + far * 2 + core for far in range(4)] for x in range(4) for core in range(2)]


def finish_kernel(
    limit, squares_ref, old_ref, parts_ref, own_ref, state_ref,
    new_ref, momentum_ref, new_buffer, momentum_buffer, new_sems, momentum_sem,
):
    depth = parts_ref.shape[1] // 2
    piece = depth // 2
    held = rate_outer * beta_outer * beta_outer
    for y in range(4):
        for half in range(2):
            for side in range(2):
                state = parts_ref[y * 2 + side, depth + half * piece : depth + (half + 1) * piece]
                start = (y * 4 + half * 2 + side) * piece
                new_buffer[start : start + piece] = old_ref[start : start + piece] - held * state
    scale = jnp.minimum(1.0, limit / jnp.sqrt(jnp.sum(squares_ref[...], keepdims=True) + epsilon))
    gain = rate_outer * (beta_outer + 1.0) * scale
    momentum_buffer[...] = beta_outer * state_ref[...] + own_ref[...] * scale
    copies = [pltpu.make_async_copy(momentum_buffer, momentum_ref, momentum_sem)]
    copies[0].start()
    for y in range(4):
        for half in range(2):
            for side in range(2):
                average = parts_ref[y * 2 + half, side * piece : (side + 1) * piece]
                start = (y * 4 + half * 2 + side) * piece
                new_buffer[start : start + piece] = new_buffer[start : start + piece] - gain * average
        chunk = pl.ds(y * 4 * piece, 4 * piece)
        copies.append(pltpu.make_async_copy(new_buffer.at[chunk], new_ref.at[chunk], new_sems.at[y]))
        copies[-1].start()
    for copy in copies:
        copy.wait()


def local(
    previous_global_weights,
    replica_local_weights,
    momentum,
    reporting_replica_tokens,
    target_fragment_index,
):
    replicas = lax.axis_size("replica")
    shards = lax.axis_size("fsdp")
    replica_pos = lax.axis_index("replica")
    row, half, side = replica_pos >> 2, (replica_pos >> 1) & 1, replica_pos & 1
    frag_total = previous_global_weights.shape[0] * shards
    limit = clip_scale * math.sqrt(frag_total)
    token_weights = reporting_replica_tokens.astype(jnp.float32)
    ones = jnp.ones((replicas, replicas), jnp.float32)
    counts = jnp.dot(token_weights[None], ones, precision=lax.Precision.HIGHEST)
    token_shares = token_weights / counts[0]
    blocks = previous_global_weights.reshape(8, -1, lanes)
    depth = blocks.shape[1]
    old_block = lax.dynamic_index_in_dim(blocks, row * 2 + side, 0, keepdims=False)
    state = lax.dynamic_index_in_dim(momentum, target_fragment_index[0], 0, keepdims=False)
    state_piece = state.reshape(-1, lanes)
    group_shares = lax.dynamic_index_in_dim(
        token_shares.reshape(4, 2, 2), half, 1, keepdims=False
    ).reshape(8)
    other_state = lax.ppermute(state_piece, "replica", [(i, i ^ 2) for i in range(replicas)])
    received = lax.all_to_all(
        replica_local_weights[0].reshape(blocks.shape),
        "replica", 0, 0, axis_index_groups=block_groups(), tiled=True,
    )
    partial = jnp.sum(group_shares[:, None, None] * (old_block[None] - received), 0)
    average = partial + lax.ppermute(partial, "replica", [(i, i ^ 2) for i in range(replicas)])
    other_state, _ = lax.optimization_barrier((other_state, partial))
    pair = jnp.stack([state_piece, other_state])
    pair = jnp.where(half == 0, pair, pair[::-1]).reshape(depth, lanes)
    beside_pair = lax.ppermute(pair, "replica", [(i, i ^ 1) for i in range(replicas)])
    near = near_groups(shards)
    squares = jnp.sum(average * average, 0, keepdims=True)
    squares = jnp.broadcast_to(squares[None], (len(near[0]), 1, lanes))
    beside = lax.ppermute(average, "replica", [(i, i ^ 1) for i in range(replicas)])
    squares = lax.all_to_all(squares, ("replica", "fsdp"), 0, 0, axis_index_groups=near, tiled=True)
    squares = jnp.sum((squares[:32, 0] + squares[32:, 0]).reshape(4, 8, lanes), 0)
    beside, squares = lax.optimization_barrier((beside, squares))
    first = side == 0
    averages = jnp.where(first, jnp.stack([average, beside]), jnp.stack([beside, average]))
    pairs = jnp.where(first, jnp.stack([pair, beside_pair]), jnp.stack([beside_pair, pair]))
    sent = jnp.concatenate([averages, pairs], 1)
    sent, squares = lax.optimization_barrier((sent, squares))
    sent = jnp.broadcast_to(sent[None], (4,) + sent.shape)
    parts = lax.all_to_all(sent, "replica", 0, 0, axis_index_groups=line_groups(), tiled=True)
    parts = parts.reshape(8, -1, lanes)
    squares = lax.psum(squares, "fsdp", axis_index_groups=far_groups())
    own = lax.dynamic_slice_in_dim(averages.reshape(-1, lanes), (replica_pos & 3) * (depth // 2), depth // 2)
    near_by = functools.partial(pltpu.with_memory_space_constraint, memory_space=pltpu.VMEM)
    vmem = pl.BlockSpec(memory_space=pltpu.VMEM)
    new_weights, new_momentum = pl.pallas_call(
        functools.partial(finish_kernel, limit),
        out_shape=(
            jax.ShapeDtypeStruct((8 * depth, lanes), jnp.float32),
            jax.ShapeDtypeStruct(state_piece.shape, jnp.float32),
        ),
        in_specs=[vmem] * 5,
        out_specs=(pl.BlockSpec(memory_space=pl.ANY), pl.BlockSpec(memory_space=pl.ANY)),
        scratch_shapes=[
            pltpu.VMEM((8 * depth, lanes), jnp.float32),
            pltpu.VMEM(state_piece.shape, jnp.float32),
            pltpu.SemaphoreType.DMA((4,)),
            pltpu.SemaphoreType.DMA,
        ],
        name="finish",
    )(near_by(squares), near_by(blocks.reshape(-1, lanes)), near_by(parts), near_by(own), near_by(state_piece))
    return (new_weights.reshape(-1), new_momentum.reshape(-1))


def solution(mesh):
    placed = (P("fsdp"), P("replica", "fsdp"), P(None, ("fsdp", "replica")), P(), P())
    return jax.shard_map(
        local,
        mesh=mesh,
        in_specs=placed,
        out_specs=(P("fsdp"), P(("fsdp", "replica"))),
        check_vma=False,
    )
```
